32 devices in a mesh: grp: 2 (over y), node: 4 (over x, core), feat: 4 (over z).
Axes of the slice: x: 2, y: 2, z: 4, core: 2. Of those that a mesh axis runs over, the one named last changes fastest.
Arguments:
- features: bfloat16 [32768, 256], P(('grp', 'node')), parts along dimension 0, may hold values from -6 to 6
- band_cols: int32 [256, 16], P(('grp', 'node', 'feat')), parts along dimension 0, may hold values from 0 to 95
- band_adj: int32 [256, 16, 128, 128], P(('grp', 'node', 'feat')), parts along dimension 0, may hold values 0 or 1
- far_cols: int32 [8, 4, 4, 3], P(('grp', 'node'), 'feat'), parts along dimension 0, may hold values from 0 to 31
- far_rows: int32 [8, 4, 4, 3], P(('grp', 'node'), 'feat'), parts along dimension 0, may hold values from 0 to 7
- far_live: int32 [8, 4, 4], P(('grp', 'node'), 'feat'), parts along dimension 0, may hold values from 0 to 3
- far_adj: int32 [8, 4, 4, 3, 128, 128], P(('grp', 'node'), 'feat'), parts along dimension 0, may hold values 0 or 1
- degree: int32 [32768], P(('grp', 'node', 'feat')), parts along dimension 0, may hold values from 16 to 128
- w_self: bfloat16 [256, 256], replicated, may hold values from -0.375 to 0.375
- w_neigh: bfloat16 [256, 256], replicated, may hold values from -1.5 to 1.5
- grad_out: bfloat16 [32768, 256], P(('grp', 'node', 'feat')), parts along dimension 0, may hold values from -6 to 6
Outputs:
- layer_out: bfloat16 [32768, 256], P(('grp', 'node', 'feat')), parts along dimension 0
- grad_features: float32 [32768, 256], P(('grp', 'node', 'feat')), parts along dimension 0
- grad_self: float32 [512, 256], P('grp'), parts along dimension 0
- grad_neigh: float32 [512, 256], P('grp'), parts along dimension 0
The draws below stay inside these ranges and needn't reach their ends.
There are 2 independent parts, one for each index of `grp`. The reference program is written for one: setup_inputs(seed, part) draws one part's arguments, and reference() takes and returns one part's arrays. A program takes and returns all parts, laid end to end along the dimension named above; an argument that names none is the same for every part. Nothing has to cross between parts.
Inputs may be any that keep to these rules, and one draw needn't show every extreme that they name: far_live[e, k, d] counts the leading slots of entry (e, k, d) that hold edges; the others are ignored.
All inputs are finite; a program needn't handle non-finite values. No bound on the sum of `band_adj` or of `far_adj` on one device may be relied on, other than what follows from the above.
Results may differ from the reference program's by a relative error of at most 0.0065.
Values may be sent and summed in bfloat16 or wider, within the bound.
A program may use at most 128 MiB of HBM per device.

```python
import jax
import jax.numpy as jnp
from jax import lax

F = 256
H = 256
TILE = 128
BAND_SLOTS = 16
FAR_SLOTS = 3
ROWS = 4096
NODES = 16384
N_NODE = 4
N_FEAT = 4


def plant(result, rng, low, high):
    longest = result.shape.index(max(result.shape))
    spots = []
    for shift in (0, 1):
        where = [jax.random.randint(jax.random.fold_in(rng, axis), (), 0, length) for axis, length in enumerate(result.shape)]
        where[longest] = (where[longest] + shift) % result.shape[longest]
        spots.append(tuple(where))
    return result.at[spots[0]].set(low).at[spots[1]].set(high)


def steps_of(key, dims, split, smallest, top_value):
    def one(axis_at, parts):
        heights = jax.random.uniform(jax.random.fold_in(jax.random.fold_in(key, 6), axis_at), (parts,), jnp.float32, smallest / len(split), top_value / len(split))
        return jnp.repeat(jnp.exp(heights), dims[axis_at] // parts).reshape((-1,) + (1,) * (len(dims) - axis_at - 1))

    gain = one(*split[0])
    for cut in split[1:]:
        gain = gain * one(*cut)
    return gain


def scatter_about(key, dims, scale, most, split=(), kind=jnp.bfloat16):
    factor_of = steps_of(key, dims, split, -0.22, 0.18) if split else 1.0
    entries = jax.random.normal(key, dims, jnp.float32) * scale * factor_of
    return jnp.minimum(jnp.maximum(entries, -most), most).astype(kind)


def setup_inputs(seed: int = 0, part: int = 0) -> dict:
    splits = jax.random.split(jax.random.key(seed), 12)
    part_keys = jax.random.split(jax.random.fold_in(splits[11], part), 12)
    return {
        "features": scatter_about(part_keys[0], (NODES, F), 1.0, 6.0, ((0, 4),)),
        "band_cols": plant(jax.random.randint(part_keys[1], (NODES // TILE, BAND_SLOTS), 0, 3 * ROWS // TILE), jax.random.fold_in(part_keys[1], 1), 0, (3 * ROWS // TILE) - 1).astype(jnp.int32),
        "band_adj": plant((jax.random.randint(part_keys[2], (NODES // TILE, BAND_SLOTS, TILE, TILE), 0, max(2, TILE // 4)) < 1).astype(jnp.int32), jax.random.fold_in(part_keys[2], 1), 0, 1),
        "far_cols": plant(jax.random.randint(part_keys[3], (N_NODE, N_FEAT, N_NODE, FAR_SLOTS), 0, ROWS // TILE), jax.random.fold_in(part_keys[3], 1), 0, (ROWS // TILE) - 1).astype(jnp.int32),
        "far_rows": plant(jax.random.randint(part_keys[4], (N_NODE, N_FEAT, N_NODE, FAR_SLOTS), 0, ROWS // (TILE * N_FEAT)), jax.random.fold_in(part_keys[4], 1), 0, (ROWS // (TILE * N_FEAT)) - 1).astype(jnp.int32),
        "far_live": plant(jax.random.randint(part_keys[5], (N_NODE, N_FEAT, N_NODE), 0, FAR_SLOTS + 1), jax.random.fold_in(part_keys[5], 1), 0, FAR_SLOTS).astype(jnp.int32),
        "far_adj": plant((jax.random.randint(part_keys[6], (N_NODE, N_FEAT, N_NODE, FAR_SLOTS, TILE, TILE), 0, max(2, TILE // 4)) < 1).astype(jnp.int32), jax.random.fold_in(part_keys[6], 1), 0, 1),
        "degree": plant(jax.random.randint(part_keys[7], (NODES,), BAND_SLOTS, 8 * BAND_SLOTS + 1), jax.random.fold_in(part_keys[7], 1), BAND_SLOTS, 8 * BAND_SLOTS).astype(jnp.int32),
        "w_self": scatter_about(splits[8], (F, H), F ** -0.5, 0.375),
        "w_neigh": scatter_about(splits[9], (F, H), (F // 16) ** -0.5, 1.5),
        "grad_out": scatter_about(part_keys[10], (NODES, H), 1.0, 6.0, ((0, 16),)),
    }


def slope_of(pre_act):
    sigmoid_z = jax.nn.sigmoid(pre_act)
    return sigmoid_z * (1.0 + pre_act * (1.0 - sigmoid_z))

def reference(features, band_cols, band_adj, far_cols, far_rows, far_live, far_adj, degree, w_self, w_neigh, grad_out):
    feat_width = features.shape[1]
    blocks = ROWS // TILE
    sub_tiles = ROWS // (TILE * N_FEAT)
    tile_count = N_NODE * blocks
    all_tiles = features.reshape(tile_count, TILE, feat_width)
    node_ids = jnp.arange(N_NODE, dtype=jnp.int32)
    col_ids = band_cols.reshape(N_NODE, blocks, BAND_SLOTS)
    near_ids = (node_ids[:, None, None] + col_ids // blocks - 1) % N_NODE * blocks + col_ids % blocks
    near_ids = near_ids.reshape(tile_count, BAND_SLOTS).astype(jnp.int32)

    def near_one(packed):
        idx_list, blocks_now = packed
        return jnp.einsum('sij,sjf->if', blocks_now.astype(jnp.float32), all_tiles[idx_list].astype(jnp.float32))
    near_sum = lax.map(near_one, (near_ids, band_adj))
    senders = jnp.arange(N_NODE * N_FEAT, dtype=jnp.int32)
    far_blocks = far_adj.reshape(N_NODE * N_FEAT, N_NODE * FAR_SLOTS, TILE, TILE)
    far_c = far_cols.reshape(N_NODE * N_FEAT, N_NODE * FAR_SLOTS)
    far_r = far_rows.reshape(N_NODE * N_FEAT, N_NODE * FAR_SLOTS)
    live_mask = jnp.arange(FAR_SLOTS, dtype=jnp.int32)[None, None, None, :] < far_live[..., None]
    live_mask = live_mask.reshape(N_NODE * N_FEAT, N_NODE * FAR_SLOTS)
    dest_node = jnp.repeat(node_ids, FAR_SLOTS)

    def far_index(sender):
        src_node = sender // N_FEAT
        member = sender % N_FEAT
        src_ids = (src_node * blocks + far_c[sender]).astype(jnp.int32)
        dst_ids = (dest_node * blocks + member * sub_tiles + far_r[sender]).astype(jnp.int32)
        return (src_ids, dst_ids)

    def far_step(running, sender):
        src_ids, dst_ids = far_index(sender)
        partial_value = jnp.einsum('pij,pjf->pif', far_blocks[sender].astype(jnp.float32), all_tiles[src_ids].astype(jnp.float32)).astype(jnp.bfloat16)
        partial_value = jnp.where(live_mask[sender][:, None, None], partial_value, jnp.zeros_like(partial_value))
        return (running.at[dst_ids].add(partial_value.astype(jnp.float32)), None)
    start = jnp.zeros((tile_count, TILE, feat_width), jnp.float32)
    far_sum, _ = lax.scan(far_step, start, senders)
    deg_f = degree.astype(jnp.float32)[:, None]
    aggregate = ((near_sum + far_sum).reshape(NODES, feat_width) / deg_f).astype(jnp.bfloat16)
    pre_act = jnp.dot(features, w_self, preferred_element_type=jnp.float32) + jnp.dot(aggregate, w_neigh, preferred_element_type=jnp.float32)
    layer_out = jax.nn.silu(pre_act).astype(jnp.bfloat16)
    grad_z = (grad_out.astype(jnp.float32) * slope_of(pre_act)).astype(jnp.bfloat16)
    grad_scale = 1.0 / jnp.sqrt(jnp.float32(NODES))
    grad_self = jnp.dot(features.T, grad_z, preferred_element_type=jnp.float32) * grad_scale
    grad_neigh = jnp.dot(aggregate.T, grad_z, preferred_element_type=jnp.float32) * grad_scale
    back_signal = (jnp.dot(grad_z, w_neigh.T, preferred_element_type=jnp.float32) / deg_f).astype(jnp.bfloat16)
    self_back = jnp.dot(grad_z, w_self.T, preferred_element_type=jnp.float32)
    back_tiles = back_signal.reshape(tile_count, TILE, feat_width)
    row_ids = jnp.arange(tile_count, dtype=jnp.int32)

    def band_back(running, row_tile):
        contrib = jnp.einsum('sij,if->sjf', band_adj[row_tile].astype(jnp.float32), back_tiles[row_tile].astype(jnp.float32))
        return (running.at[near_ids[row_tile]].add(contrib), None)
    spread, _ = lax.scan(band_back, start, row_ids)

    def far_back(running, sender):
        src_ids, dst_ids = far_index(sender)
        contrib = jnp.einsum('pij,pif->pjf', far_blocks[sender].astype(jnp.float32), back_tiles[dst_ids].astype(jnp.float32))
        contrib = jnp.where(live_mask[sender][:, None, None], contrib, jnp.zeros_like(contrib))
        return (running.at[src_ids].add(contrib), None)
    spread, _ = lax.scan(far_back, spread, senders)
    grad_features = self_back + spread.reshape(NODES, feat_width)
    return (layer_out, grad_features, grad_self, grad_neigh)
```

```python
import functools
import math

import jax
import jax.numpy as jnp
from jax import lax
from jax.experimental import pallas as pl
from jax.experimental.pallas import tpu as pltpu
from jax.sharding import PartitionSpec as P

F32 = jnp.float32
BF16 = jnp.bfloat16


def outer(a, b):
    return lax.dot_general(a, b, (((0,), (0,)), ((), ())), preferred_element_type=F32)


def times_t(a, b):
    return lax.dot_general(a, b, (((1,), (1,)), ((), ())), preferred_element_type=F32)


def far_kernel(slots, cols, live, feat_ref, adj_ref, out_ref):
    p = pl.program_id(0)
    for s in range(slots):
        value = jnp.dot(
            adj_ref[0, s].astype(BF16), feat_ref[cols[p, s]], preferred_element_type=F32
        )
        out_ref[0, s] = jnp.where(s < live[p], value, 0.0).astype(BF16)


def main_kernel(
    dims,
    cols,
    rows,
    spot,
    own_hbm,
    in_hbm,
    *rest,
):
    blocks, slots, n_cross, n_feat, n_far, n_parts = dims
    cross_hbm, rest = rest[:n_cross], rest[n_cross:]
    part_refs, rest = rest[:n_parts], rest[n_parts:]
    adj_ref, deg_ref, ws_ref, wn_ref, go_ref = rest[:5]
    rest = rest[5:]
    out_ref, self_ref, gs_ref, gn_ref, own_ref, in_ref = rest[:6]
    rest = rest[6:]
    cross_refs, rest = rest[:n_feat], rest[n_feat:]
    send_refs, rest = rest[:n_parts], rest[n_parts:]
    ext, wide, back, acc, sems = rest
    t = pl.program_id(0)
    last = pl.num_programs(0) - 1
    sub = blocks // n_feat

    @pl.when(t == 0)
    def _():
        moves = [
            pltpu.make_async_copy(own_hbm, ext.at[pl.ds(0, blocks)], sems.at[0]),
            pltpu.make_async_copy(in_hbm, ext.at[pl.ds(blocks, blocks)], sems.at[1]),
        ]
        each = blocks // n_cross
        for i, ref in enumerate(cross_hbm):
            moves.append(
                pltpu.make_async_copy(ref, ext.at[pl.ds(2 * blocks + i * each, each)], sems.at[2 + i])
            )
        for move in moves:
            move.start()
        wide[...] = jnp.zeros_like(wide)
        gs_ref[...] = jnp.zeros_like(gs_ref)
        gn_ref[...] = jnp.zeros_like(gn_ref)
        for move in moves:
            move.wait()

    adj = [adj_ref[0, s].astype(BF16) for s in range(slots)]
    near = None
    for s in range(0, slots, 2):
        left = jnp.concatenate([adj[s], adj[s + 1]], axis=1)
        right = jnp.concatenate([ext[cols[t, s]], ext[cols[t, s + 1]]], axis=0)
        term = jnp.dot(left, right, preferred_element_type=F32)
        near = term if near is None else near + term
    acc[...] = near
    for k, ref in enumerate(part_refs):
        for s in range(n_far):

            @pl.when(rows[k, s] == t)
            def _():
                acc[...] += ref[s].astype(F32)

    deg = jnp.broadcast_to(deg_ref[0].astype(F32), (deg_ref.shape[2], deg_ref.shape[2])).T
    deg = jnp.concatenate([deg, deg], axis=1)
    agg = (acc[...] / deg).astype(BF16)
    mine = ext[spot[0] + t]
    pre = jnp.dot(mine, ws_ref[...], preferred_element_type=F32) + jnp.dot(
        agg, wn_ref[...], preferred_element_type=F32
    )
    sig = jax.nn.sigmoid(pre)
    out_ref[...] = (pre * sig).astype(BF16)
    gz = (go_ref[...].astype(F32) * (sig * (1.0 + pre * (1.0 - sig)))).astype(BF16)
    gs_ref[...] += outer(mine, gz)
    gn_ref[...] += outer(agg, gz)
    bk = (times_t(gz, wn_ref[...]) / deg).astype(BF16)
    self_ref[...] = times_t(gz, ws_ref[...])
    back[t] = bk
    for s in range(slots):
        wide[cols[t, s]] += outer(adj[s], bk)

    @pl.when(t == last)
    def _():
        own_ref[...] = wide[pl.ds(0, blocks)]
        in_ref[...] = wide[pl.ds(blocks, blocks)].astype(BF16)
        for d in range(n_feat):
            cross_refs[d][...] = wide[pl.ds(spot[1 + d], sub)].astype(BF16)
        for k in range(n_parts):
            for s in range(n_far):
                send_refs[k][s] = back[rows[k, s]]


def join_kernel(slots, n_parts, cols, live, own_ref, in_ref, adj_ref, *rest):
    ret_refs, out_ref = rest[:n_parts], rest[n_parts]
    out_ref[...] = own_ref[...] + in_ref[...].astype(F32)
    for k in range(n_parts):
        for s in range(slots):

            @pl.when(s < live[k])
            def _():
                out_ref[cols[k, s]] += outer(adj_ref[k, s].astype(BF16), ret_refs[k][s])


def shards(
    features,
    band_cols,
    band_adj,
    far_cols,
    far_rows,
    far_live,
    far_adj,
    degree,
    w_self,
    w_neigh,
    grad_out,
):
    block_rows, width = features.shape
    sub_tiles, slots, tile, _ = band_adj.shape
    hidden = w_self.shape[1]
    blocks = block_rows // tile
    n_feat = lax.axis_size("feat")
    n_node = lax.axis_size("node")
    far_slots = far_adj.shape[3]
    sub_rows = sub_tiles * tile
    half = blocks // 2
    node = lax.axis_index("node")
    member = lax.axis_index("feat")
    h = member % 2
    even = node % 2 == 0
    in_pairs = [(i, i ^ 1) for i in range(n_node)]
    cross_of = [(i + 1) % n_node if i % 2 else (i - 1) % n_node for i in range(n_node)]
    cross_pairs = list(enumerate(cross_of))
    feat_pairs = [(i, i ^ 1) for i in range(n_feat)]

    def dist(k):
        return [(i, (i + k) % n_node) for i in range(n_node)]

    tiles = features.reshape(blocks, tile, width)
    order = (node + jnp.arange(n_node, dtype=jnp.int32)) % n_node
    far_c = far_cols.reshape(n_node, far_slots)[order]
    far_r = far_rows.reshape(n_node, far_slots)[order]
    live = far_live.reshape(n_node)[order]
    fadj = far_adj.reshape(n_node, far_slots, tile, tile)
    got_rows = [far_r[0]] + [lax.ppermute(far_r[k], "node", dist(k)) for k in range(1, n_node)]
    rows = jnp.stack(got_rows)

    from_in = lax.ppermute(tiles, "node", in_pairs)
    n_pieces = 2
    each = half // n_pieces
    direct, relayed = [], []
    for i in range(n_pieces):
        piece = lax.dynamic_slice_in_dim(tiles, h * half + i * each, each, 0)
        direct.append(lax.ppermute(piece, "node", cross_pairs))
    for piece in direct:
        relayed.append(lax.ppermute(piece, "feat", feat_pairs))

    far_fn = pl.pallas_call(
        lambda c, l, o, f, a, out: far_kernel(far_slots, c, l, f, a, out),
        out_shape=jax.ShapeDtypeStruct((n_node, far_slots, tile, width), BF16),
        grid_spec=pltpu.PrefetchScalarGridSpec(
            num_scalar_prefetch=3,
            grid=(n_node,),
            in_specs=[
                pl.BlockSpec((blocks, tile, width), lambda p, c, l, o: (0, 0, 0)),
                pl.BlockSpec((1, far_slots, tile, tile), lambda p, c, l, o: (o[p], 0, 0, 0)),
            ],
            out_specs=pl.BlockSpec((1, far_slots, tile, width), lambda p, c, l, o: (p, 0, 0, 0)),
        ),
        compiler_params=pltpu.CompilerParams(vmem_limit_bytes=32 * 1024 * 1024),
        name="far_partial",
    )
    parts = far_fn(far_c, live, order, tiles, fadj)
    got = [parts[0]] + [lax.ppermute(parts[k], "node", dist(k)) for k in range(1, n_node)]

    kind, local = band_cols // blocks, band_cols % blocks
    is_in = kind == jnp.where(even, 2, 0)
    cross_place = 2 * blocks + ((local // half) ^ h) * half + local % half
    place = jnp.where(kind == 1, local, jnp.where(is_in, blocks + local, cross_place))
    spots = [member * sub_tiles]
    for d in range(n_feat):
        first = (member ^ d) * sub_tiles
        spots.append(2 * blocks + ((first // half) ^ h) * half + first % half)
    spot = jnp.stack(spots).astype(jnp.int32)

    cross_in = direct + relayed
    n_cross = len(cross_in)
    vmem = lambda shape: pl.BlockSpec(shape, lambda t, *_: (0,) * len(shape))
    any_spec = pl.BlockSpec(memory_space=pl.ANY)
    far_shape = (far_slots, tile, width)
    dims = (blocks, slots, n_cross, n_feat, far_slots, n_node)
    results = pl.pallas_call(
        functools.partial(main_kernel, dims),
        out_shape=[
            jax.ShapeDtypeStruct((sub_rows, hidden), BF16),
            jax.ShapeDtypeStruct((sub_rows, width), F32),
            jax.ShapeDtypeStruct((width, hidden), F32),
            jax.ShapeDtypeStruct((width, hidden), F32),
            jax.ShapeDtypeStruct((blocks, tile, width), F32),
            jax.ShapeDtypeStruct((blocks, tile, width), BF16),
        ]
        + [jax.ShapeDtypeStruct((sub_tiles, tile, width), BF16)] * n_feat
        + [jax.ShapeDtypeStruct(far_shape, BF16)] * n_node,
        grid_spec=pltpu.PrefetchScalarGridSpec(
            num_scalar_prefetch=3,
            grid=(sub_tiles,),
            in_specs=[any_spec] * (2 + n_cross)
            + [vmem(far_shape)] * n_node
            + [
                pl.BlockSpec((1, slots, tile, tile), lambda t, *_: (t, 0, 0, 0)),
                pl.BlockSpec((1, 1, tile), lambda t, *_: (t, 0, 0)),
                vmem((width, hidden)),
                vmem((width, hidden)),
                pl.BlockSpec((tile, hidden), lambda t, *_: (t, 0)),
            ],
            out_specs=[
                pl.BlockSpec((tile, hidden), lambda t, *_: (t, 0)),
                pl.BlockSpec((tile, width), lambda t, *_: (t, 0)),
                vmem((width, hidden)),
                vmem((width, hidden)),
                vmem((blocks, tile, width)),
                vmem((blocks, tile, width)),
            ]
            + [vmem((sub_tiles, tile, width))] * n_feat
            + [vmem(far_shape)] * n_node,
            scratch_shapes=[
                pltpu.VMEM((3 * blocks, tile, width), BF16),
                pltpu.VMEM((3 * blocks, tile, width), F32),
                pltpu.VMEM((sub_tiles, tile, width), BF16),
                pltpu.VMEM((tile, width), F32),
                pltpu.SemaphoreType.DMA((2 + n_cross,)),
            ],
        ),
        compiler_params=pltpu.CompilerParams(vmem_limit_bytes=58 * 1024 * 1024),
        name="layer",
    )(
        place,
        rows,
        spot,
        tiles,
        from_in,
        *cross_in,
        *got,
        band_adj,
        degree.reshape(sub_tiles, 1, tile),
        w_self,
        w_neigh,
        grad_out,
    )
    layer_out, self_back, part_self, part_neigh, own_wide, in_wide = results[:6]
    cross_wide = results[6 : 6 + n_feat]
    send_back = results[6 + n_feat :]

    returned = [send_back[0]] + [
        lax.ppermute(send_back[k], "node", dist(n_node - k)) for k in range(1, n_node)
    ]
    in_terms = lax.ppermute(in_wide, "node", in_pairs)
    far_first = list(range(n_feat - 1, -1, -1))
    cross_terms = {d: lax.ppermute(cross_wide[d], "node", cross_pairs) for d in far_first}
    sum_self, sum_neigh = lax.psum((part_self, part_neigh), ("node", "feat"))
    grad_scale = 1.0 / math.sqrt(block_rows * n_node)

    base = pl.pallas_call(
        functools.partial(join_kernel, far_slots, n_node),
        out_shape=jax.ShapeDtypeStruct((blocks, tile, width), F32),
        in_specs=[pl.BlockSpec(memory_space=pltpu.SMEM)] * 2
        + [pl.BlockSpec(memory_space=pltpu.VMEM)] * (3 + n_node),
        out_specs=pl.BlockSpec(memory_space=pltpu.VMEM),
        compiler_params=pltpu.CompilerParams(vmem_limit_bytes=40 * 1024 * 1024),
        name="join",
    )(far_c, live, own_wide, in_terms, fadj[order], *returned)

    total = self_back
    for d in far_first:
        chunk = lax.dynamic_slice_in_dim(base, (member ^ d) * sub_tiles, sub_tiles, 0)
        chunk = (chunk + cross_terms[d].astype(F32)).astype(BF16)
        if d:
            chunk = lax.ppermute(chunk, "feat", [(i, i ^ d) for i in range(n_feat)])
        total = total + chunk.reshape(sub_rows, width).astype(F32)
    return (layer_out, total, sum_self * grad_scale, sum_neigh * grad_scale)


def solution(mesh):
    placed = (
        P(("grp", "node"), None),
        P(("grp", "node", "feat"), None),
        P(("grp", "node", "feat"), None, None, None),
        P(("grp", "node"), "feat", None, None),
        P(("grp", "node"), "feat", None, None),
        P(("grp", "node"), "feat", None),
        P(("grp", "node"), "feat", None, None, None, None),
        P(("grp", "node", "feat")),
        P(),
        P(),
        P(("grp", "node", "feat"), None),
    )
    return jax.shard_map(
        shards,
        mesh=mesh,
        in_specs=placed,
        out_specs=(
            P(("grp", "node", "feat"), None),
            P(("grp", "node", "feat"), None),
            P("grp", None),
            P("grp", None),
        ),
        check_vma=False,
    )
```

```python
import functools
import math

import jax
import jax.numpy as jnp
from jax import lax
from jax.experimental import pallas as pl
from jax.experimental.pallas import tpu as pltpu
from jax.sharding import PartitionSpec as P

F32 = jnp.float32
BF16 = jnp.bfloat16


def outer(a, b):
    return lax.dot_general(a, b, (((0,), (0,)), ((), ())), preferred_element_type=F32)


def times_t(a, b):
    return lax.dot_general(a, b, (((1,), (1,)), ((), ())), preferred_element_type=F32)


def far_kernel(slots, n_node, cols, rows, live, node, feat_ref, adj_ref, *outs):
    tile, width = feat_ref.shape[1:]
    for k, out_ref in enumerate(outs):
        p = lax.rem(node[0] + k, n_node)
        for s in range(slots):
            value = jnp.dot(
                adj_ref[p, s].astype(BF16), feat_ref[cols[p, s]], preferred_element_type=F32
            )
            out_ref[s * tile : (s + 1) * tile] = jnp.where(s < live[p], value, 0.0).astype(BF16)
        line = lax.broadcasted_iota(jnp.int32, (16, width), 0)
        named = jnp.zeros((16, width), F32)
        for s in range(slots):
            named = jnp.where(line == s, rows[p, s].astype(F32), named)
        out_ref[slots * tile :] = named.astype(BF16)


def main_kernel(
    dims,
    cols,
    rows,
    spot,
    own_hbm,
    in_hbm,
    *rest,
):
    blocks, slots, n_cross, n_feat, n_far, n_parts = dims
    cross_hbm, rest = rest[:n_cross], rest[n_cross:]
    part_refs, rest = rest[:n_parts], rest[n_parts:]
    adj_ref, deg_ref, ws_ref, wn_ref, go_ref = rest[:5]
    rest = rest[5:]
    out_ref, self_ref, gs_ref, gn_ref, own_ref, in_ref = rest[:6]
    rest = rest[6:]
    cross_refs, rest = rest[:n_feat], rest[n_feat:]
    send_refs, rest = rest[:n_parts], rest[n_parts:]
    ext, wide, back, acc, sems = rest
    t = pl.program_id(0)
    last = pl.num_programs(0) - 1
    sub = blocks // n_feat

    @pl.when(t == 0)
    def _():
        moves = [
            pltpu.make_async_copy(own_hbm, ext.at[pl.ds(0, blocks)], sems.at[0]),
            pltpu.make_async_copy(in_hbm, ext.at[pl.ds(blocks, blocks)], sems.at[1]),
        ]
        each = blocks // n_cross
        for i, ref in enumerate(cross_hbm):
            moves.append(
                pltpu.make_async_copy(ref, ext.at[pl.ds(2 * blocks + i * each, each)], sems.at[2 + i])
            )
        for move in moves:
            move.start()
        wide[...] = jnp.zeros_like(wide)
        gs_ref[...] = jnp.zeros_like(gs_ref)
        gn_ref[...] = jnp.zeros_like(gn_ref)
        for move in moves:
            move.wait()

    adj = [adj_ref[0, s].astype(BF16) for s in range(slots)]
    near = None
    for s in range(0, slots, 2):
        left = jnp.concatenate([adj[s], adj[s + 1]], axis=1)
        right = jnp.concatenate([ext[cols[t, s]], ext[cols[t, s + 1]]], axis=0)
        term = jnp.dot(left, right, preferred_element_type=F32)
        near = term if near is None else near + term
    acc[...] = near
    for k, ref in enumerate(part_refs):
        for s in range(n_far):

            @pl.when(rows[k, s] == t)
            def _():
                acc[...] += ref[s * acc.shape[0] : (s + 1) * acc.shape[0]].astype(F32)

    deg = jnp.broadcast_to(deg_ref[0].astype(F32), (deg_ref.shape[2], deg_ref.shape[2])).T
    deg = jnp.concatenate([deg, deg], axis=1)
    agg = (acc[...] / deg).astype(BF16)
    mine = ext[spot[0] + t]
    pre = jnp.dot(mine, ws_ref[...], preferred_element_type=F32) + jnp.dot(
        agg, wn_ref[...], preferred_element_type=F32
    )
    sig = jax.nn.sigmoid(pre)
    out_ref[...] = (pre * sig).astype(BF16)
    gz = (go_ref[...].astype(F32) * (sig * (1.0 + pre * (1.0 - sig)))).astype(BF16)
    gs_ref[...] += outer(mine, gz)
    gn_ref[...] += outer(agg, gz)
    bk = (times_t(gz, wn_ref[...]) / deg).astype(BF16)
    self_ref[...] = times_t(gz, ws_ref[...])
    back[t] = bk
    for s in range(slots):
        wide[cols[t, s]] += outer(adj[s], bk)

    @pl.when(t == last)
    def _():
        own_ref[...] = wide[pl.ds(0, blocks)]
        in_ref[...] = wide[pl.ds(blocks, blocks)].astype(BF16)
        for d in range(n_feat):
            cross_refs[d][...] = wide[pl.ds(spot[1 + d], sub)].astype(BF16)
        for k in range(n_parts):
            for s in range(n_far):
                send_refs[k][s] = back[rows[k, s]]


def join_kernel(slots, n_parts, cols, live, node, own_ref, in_ref, adj_ref, *rest):
    ret_refs, out_ref = rest[:n_parts], rest[n_parts]
    out_ref[...] = own_ref[...] + in_ref[...].astype(F32)
    for k in range(n_parts):
        p = lax.rem(node[0] + k, n_parts)
        for s in range(slots):

            @pl.when(s < live[p])
            def _():
                out_ref[cols[p, s]] += outer(adj_ref[p, s].astype(BF16), ret_refs[k][s])


def summed(value, node, member, n_node, n_feat):
    rounds = [("node", node, n_node), ("feat", member, n_feat)]
    for axis, at, size in rounds:
        half = value.shape[0] // 2
        bit = at % 2
        pairs = [(i, i ^ 1) for i in range(size)]
        away = lax.dynamic_slice_in_dim(value, (1 - bit) * half, half, 0)
        kept = lax.dynamic_slice_in_dim(value, bit * half, half, 0)
        value = kept + lax.ppermute(away, axis, pairs)
    for axis, size in (("feat", n_feat), ("node", n_node)):
        step = 2
        while step < size:
            value = value + lax.ppermute(value, axis, [(i, i ^ step) for i in range(size)])
            step *= 2
    for axis, at, size in rounds[::-1]:
        other = lax.ppermute(value, axis, [(i, i ^ 1) for i in range(size)])
        first = at % 2 == 0
        value = jnp.concatenate(
            [jnp.where(first, value, other), jnp.where(first, other, value)], axis=0
        )
    return value


def shards(
    features,
    band_cols,
    band_adj,
    far_cols,
    far_rows,
    far_live,
    far_adj,
    degree,
    w_self,
    w_neigh,
    grad_out,
):
    block_rows, width = features.shape
    sub_tiles, slots, tile, _ = band_adj.shape
    hidden = w_self.shape[1]
    blocks = block_rows // tile
    n_feat = lax.axis_size("feat")
    n_node = lax.axis_size("node")
    far_slots = far_adj.shape[3]
    sub_rows = sub_tiles * tile
    half = blocks // 2
    node = lax.axis_index("node")
    member = lax.axis_index("feat")
    h = member % 2
    even = node % 2 == 0
    in_pairs = [(i, i ^ 1) for i in range(n_node)]
    cross_of = [(i + 1) % n_node if i % 2 else (i - 1) % n_node for i in range(n_node)]
    cross_pairs = list(enumerate(cross_of))
    feat_pairs = [(i, i ^ 1) for i in range(n_feat)]

    def dist(k):
        return [(i, (i + k) % n_node) for i in range(n_node)]

    tiles = features.reshape(blocks, tile, width)
    far_c = far_cols.reshape(n_node, far_slots)
    far_r = far_rows.reshape(n_node, far_slots)
    live = far_live.reshape(n_node)
    fadj = far_adj.reshape(n_node, far_slots, tile, tile)
    here = node.reshape(1)
    smem = pl.BlockSpec(memory_space=pltpu.SMEM)
    whole = pl.BlockSpec(memory_space=pltpu.VMEM)

    far_len = -(-far_slots // 16) * 16 + far_slots * tile
    parts = pl.pallas_call(
        functools.partial(far_kernel, far_slots, n_node),
        out_shape=[jax.ShapeDtypeStruct((far_len, width), BF16)] * n_node,
        in_specs=[smem] * 4 + [whole] * 2,
        out_specs=[whole] * n_node,
        compiler_params=pltpu.CompilerParams(vmem_limit_bytes=32 * 1024 * 1024),
        name="far_partial",
    )(far_c, far_r, live, here, tiles, fadj)
    got = [parts[0]] + [lax.ppermute(parts[k], "node", dist(k)) for k in range(1, n_node)]
    rows = jnp.stack(
        [g[far_slots * tile : far_slots * tile + far_slots, 0].astype(jnp.int32) for g in got]
    )

    from_in = lax.ppermute(tiles, "node", in_pairs)
    n_pieces = 2
    each = half // n_pieces
    direct, relayed = [], []
    for i in range(n_pieces):
        piece = lax.dynamic_slice_in_dim(tiles, h * half + i * each, each, 0)
        if i:
            piece, _ = lax.optimization_barrier((piece, parts[0]))
        direct.append(lax.ppermute(piece, "node", cross_pairs))
    for piece in direct:
        relayed.append(lax.ppermute(piece, "feat", feat_pairs))

    kind, local = band_cols // blocks, band_cols % blocks
    is_in = kind == jnp.where(even, 2, 0)
    cross_place = 2 * blocks + ((local // half) ^ h) * half + local % half
    place = jnp.where(kind == 1, local, jnp.where(is_in, blocks + local, cross_place))
    spots = [member * sub_tiles]
    for d in range(n_feat):
        first = (member ^ d) * sub_tiles
        spots.append(2 * blocks + ((first // half) ^ h) * half + first % half)
    spot = jnp.stack(spots).astype(jnp.int32)

    cross_in = direct + relayed
    n_cross = len(cross_in)
    vmem = lambda shape: pl.BlockSpec(shape, lambda t, *_: (0,) * len(shape))
    any_spec = pl.BlockSpec(memory_space=pl.ANY)
    far_shape = (far_slots, tile, width)
    dims = (blocks, slots, n_cross, n_feat, far_slots, n_node)
    results = pl.pallas_call(
        functools.partial(main_kernel, dims),
        out_shape=[
            jax.ShapeDtypeStruct((sub_rows, hidden), BF16),
            jax.ShapeDtypeStruct((sub_rows, width), F32),
            jax.ShapeDtypeStruct((width, hidden), F32),
            jax.ShapeDtypeStruct((width, hidden), F32),
            jax.ShapeDtypeStruct((blocks, tile, width), F32),
            jax.ShapeDtypeStruct((blocks, tile, width), BF16),
        ]
        + [jax.ShapeDtypeStruct((sub_tiles, tile, width), BF16)] * n_feat
        + [jax.ShapeDtypeStruct(far_shape, BF16)] * n_node,
        grid_spec=pltpu.PrefetchScalarGridSpec(
            num_scalar_prefetch=3,
            grid=(sub_tiles,),
            in_specs=[any_spec] * (2 + n_cross)
            + [vmem((far_len, width))] * n_node
            + [
                pl.BlockSpec((1, slots, tile, tile), lambda t, *_: (t, 0, 0, 0)),
                pl.BlockSpec((1, 1, tile), lambda t, *_: (t, 0, 0)),
                vmem((width, hidden)),
                vmem((width, hidden)),
                pl.BlockSpec((tile, hidden), lambda t, *_: (t, 0)),
            ],
            out_specs=[
                pl.BlockSpec((tile, hidden), lambda t, *_: (t, 0)),
                pl.BlockSpec((tile, width), lambda t, *_: (t, 0)),
                vmem((width, hidden)),
                vmem((width, hidden)),
                vmem((blocks, tile, width)),
                vmem((blocks, tile, width)),
            ]
            + [vmem((sub_tiles, tile, width))] * n_feat
            + [vmem(far_shape)] * n_node,
            scratch_shapes=[
                pltpu.VMEM((3 * blocks, tile, width), BF16),
                pltpu.VMEM((3 * blocks, tile, width), F32),
                pltpu.VMEM((sub_tiles, tile, width), BF16),
                pltpu.VMEM((tile, width), F32),
                pltpu.SemaphoreType.DMA((2 + n_cross,)),
            ],
        ),
        compiler_params=pltpu.CompilerParams(vmem_limit_bytes=58 * 1024 * 1024),
        name="layer",
    )(
        place,
        rows,
        spot,
        tiles,
        from_in,
        *cross_in,
        *got,
        band_adj,
        degree.reshape(sub_tiles, 1, tile),
        w_self,
        w_neigh,
        grad_out,
    )
    layer_out, self_back, part_self, part_neigh, own_wide, in_wide = results[:6]
    cross_wide = results[6 : 6 + n_feat]
    send_back = results[6 + n_feat :]

    returned = [send_back[0]] + [
        lax.ppermute(send_back[k], "node", dist(n_node - k)) for k in range(1, n_node)
    ]
    in_terms = lax.ppermute(in_wide, "node", in_pairs)
    odd_first = sorted(range(n_feat), key=lambda d: ((d & -d) if d else n_feat, -d))
    cross_terms = {}
    for d in odd_first:
        outgoing = cross_wide[d]
        if d % 2 == 0:
            outgoing, _ = lax.optimization_barrier((outgoing, in_terms if d == 0 else returned[1]))
        cross_terms[d] = lax.ppermute(outgoing, "node", cross_pairs)
    grad_scale = 1.0 / math.sqrt(block_rows * n_node)
    both, _ = lax.optimization_barrier(
        (jnp.concatenate([part_self, part_neigh], 0), returned[n_node - 1])
    )
    both = summed(both, node, member, n_node, n_feat)
    both = both * grad_scale

    base = pl.pallas_call(
        functools.partial(join_kernel, far_slots, n_node),
        out_shape=jax.ShapeDtypeStruct((blocks, tile, width), F32),
        in_specs=[smem] * 3
        + [pl.BlockSpec(memory_space=pltpu.VMEM)] * (3 + n_node),
        out_specs=pl.BlockSpec(memory_space=pltpu.VMEM),
        compiler_params=pltpu.CompilerParams(vmem_limit_bytes=40 * 1024 * 1024),
        name="join",
    )(far_c, live, here, own_wide, in_terms, fadj, *returned)

    total = self_back.reshape(sub_tiles, tile, width)
    extra = [[] for _ in range(n_feat)]
    sent = None
    for d in odd_first:
        cross = cross_terms[d]
        if sent is not None:
            cross, _ = lax.optimization_barrier((cross, sent))
        chunk = lax.dynamic_slice_in_dim(base, (member ^ d) * sub_tiles, sub_tiles, 0)
        chunk = chunk + cross.astype(F32)
        for term in extra[d]:
            chunk = chunk + term.astype(F32)
        if d == 0:
            total = total + chunk
            break
        sent = chunk.astype(BF16)
        step = d & -d
        extra[d ^ step].append(
            lax.ppermute(sent, "feat", [(i, i ^ step) for i in range(n_feat)])
        )
    return (
        layer_out,
        total.reshape(sub_rows, width),
        both[:width],
        both[width:],
    )


def solution(mesh):
    placed = (
        P(("grp", "node"), None),
        P(("grp", "node", "feat"), None),
        P(("grp", "node", "feat"), None, None, None),
        P(("grp", "node"), "feat", None, None),
        P(("grp", "node"), "feat", None, None),
        P(("grp", "node"), "feat", None),
        P(("grp", "node"), "feat", None, None, None, None),
        P(("grp", "node", "feat")),
        P(),
        P(),
        P(("grp", "node", "feat"), None),
    )
    return jax.shard_map(
        shards,
        mesh=mesh,
        in_specs=placed,
        out_specs=(
            P(("grp", "node", "feat"), None),
            P(("grp", "node", "feat"), None),
            P("grp", None),
            P("grp", None),
        ),
        check_vma=False,
    )
```

```python
import functools
import math

import jax
import jax.numpy as jnp
from jax import lax
from jax.experimental import pallas as pl
from jax.experimental.pallas import tpu as pltpu
from jax.sharding import PartitionSpec as P

F32 = jnp.float32
BF16 = jnp.bfloat16


def outer(a, b):
    return lax.dot_general(a, b, (((0,), (0,)), ((), ())), preferred_element_type=F32)


def times_t(a, b):
    return lax.dot_general(a, b, (((1,), (1,)), ((), ())), preferred_element_type=F32)


def far_kernel(slots, n_node, cols, rows, live, node, feat_ref, adj_ref, *outs):
    tile, width = feat_ref.shape[1:]
    for k, out_ref in enumerate(outs):
        p = lax.rem(node[0] + k, n_node)
        for s in range(slots):
            value = jnp.dot(
                adj_ref[p, s].astype(BF16), feat_ref[cols[p, s]], preferred_element_type=F32
            )
            out_ref[s * tile : (s + 1) * tile] = jnp.where(s < live[p], value, 0.0).astype(BF16)
        line = lax.broadcasted_iota(jnp.int32, (16, width), 0)
        named = jnp.zeros((16, width), F32)
        for s in range(slots):
            named = jnp.where(line == s, rows[p, s].astype(F32), named)
        out_ref[slots * tile :] = named.astype(BF16)


def main_kernel(
    dims,
    cols,
    rows,
    spot,
    own_hbm,
    in_hbm,
    *rest,
):
    blocks, slots, n_cross, n_feat, n_far, n_parts = dims
    cross_hbm, rest = rest[:n_cross], rest[n_cross:]
    part_refs, rest = rest[:n_parts], rest[n_parts:]
    adj_ref, deg_ref, ws_ref, wn_ref, go_ref = rest[:5]
    rest = rest[5:]
    out_ref, self_ref, gs_ref, gn_ref, own_ref, in_ref = rest[:6]
    rest = rest[6:]
    cross_refs, rest = rest[:n_feat], rest[n_feat:]
    send_refs, rest = rest[:n_parts], rest[n_parts:]
    ext, wide, back, acc, sems = rest
    t = pl.program_id(0)
    last = pl.num_programs(0) - 1
    sub = blocks // n_feat

    @pl.when(t == 0)
    def _():
        moves = [
            pltpu.make_async_copy(own_hbm, ext.at[pl.ds(0, blocks)], sems.at[0]),
            pltpu.make_async_copy(in_hbm, ext.at[pl.ds(blocks, blocks)], sems.at[1]),
        ]
        each = blocks // n_cross
        for i, ref in enumerate(cross_hbm):
            moves.append(
                pltpu.make_async_copy(ref, ext.at[pl.ds(2 * blocks + i * each, each)], sems.at[2 + i])
            )
        for move in moves:
            move.start()
        wide[...] = jnp.zeros_like(wide)
        gs_ref[...] = jnp.zeros_like(gs_ref)
        gn_ref[...] = jnp.zeros_like(gn_ref)
        for move in moves:
            move.wait()

    adj = [adj_ref[0, s].astype(BF16) for s in range(slots)]
    near = None
    for s in range(0, slots, 2):
        left = jnp.concatenate([adj[s], adj[s + 1]], axis=1)
        right = jnp.concatenate([ext[cols[t, s]], ext[cols[t, s + 1]]], axis=0)
        term = jnp.dot(left, right, preferred_element_type=F32)
        near = term if near is None else near + term
    acc[...] = near
    for k, ref in enumerate(part_refs):
        for s in range(n_far):

            @pl.when(rows[k, s] == t)
            def _():
                acc[...] += ref[s * acc.shape[0] : (s + 1) * acc.shape[0]].astype(F32)

    deg = jnp.broadcast_to(deg_ref[0].astype(F32), (deg_ref.shape[2], deg_ref.shape[2])).T
    deg = jnp.concatenate([deg, deg], axis=1)
    agg = (acc[...] / deg).astype(BF16)
    mine = ext[spot[0] + t]
    pre = jnp.dot(mine, ws_ref[...], preferred_element_type=F32) + jnp.dot(
        agg, wn_ref[...], preferred_element_type=F32
    )
    sig = jax.nn.sigmoid(pre)
    out_ref[...] = (pre * sig).astype(BF16)
    gz = (go_ref[...].astype(F32) * (sig * (1.0 + pre * (1.0 - sig)))).astype(BF16)
    gs_ref[...] += outer(mine, gz)
    gn_ref[...] += outer(agg, gz)
    bk = (times_t(gz, wn_ref[...]) / deg).astype(BF16)
    self_ref[...] = times_t(gz, ws_ref[...])
    back[t] = bk
    for s in range(slots):
        wide[cols[t, s]] += outer(adj[s], bk)

    @pl.when(t == last)
    def _():
        own_ref[...] = wide[pl.ds(0, blocks)]
        in_ref[...] = wide[pl.ds(blocks, blocks)].astype(BF16)
        for d in range(n_feat):
            cross_refs[d][...] = wide[pl.ds(spot[1 + d], sub)].astype(BF16)
        for k in range(n_parts):
            for s in range(n_far):
                send_refs[k][s] = back[rows[k, s]]


def join_kernel(slots, n_parts, cols, live, node, own_ref, in_ref, adj_ref, *rest):
    ret_refs, out_ref = rest[:n_parts], rest[n_parts]
    out_ref[...] = own_ref[...] + in_ref[...].astype(F32)
    for k in range(n_parts):
        p = lax.rem(node[0] + k, n_parts)
        for s in range(slots):

            @pl.when(s < live[p])
            def _():
                out_ref[cols[p, s]] += outer(adj_ref[p, s].astype(BF16), ret_refs[k][s])


def summed(value, node, member, n_node, n_feat):
    rounds = [("node", node, n_node), ("feat", member, n_feat)]
    for axis, at, size in rounds:
        half = value.shape[0] // 2
        bit = at % 2
        pairs = [(i, i ^ 1) for i in range(size)]
        away = lax.dynamic_slice_in_dim(value, (1 - bit) * half, half, 0)
        kept = lax.dynamic_slice_in_dim(value, bit * half, half, 0)
        value = kept + lax.ppermute(away, axis, pairs)
    for axis, size in (("feat", n_feat), ("node", n_node)):
        step = 2
        while step < size:
            value = value + lax.ppermute(value, axis, [(i, i ^ step) for i in range(size)])
            step *= 2
    for axis, at, size in rounds[::-1]:
        other = lax.ppermute(value, axis, [(i, i ^ 1) for i in range(size)])
        first = at % 2 == 0
        value = jnp.concatenate(
            [jnp.where(first, value, other), jnp.where(first, other, value)], axis=0
        )
    return value


def shards(
    features,
    band_cols,
    band_adj,
    far_cols,
    far_rows,
    far_live,
    far_adj,
    degree,
    w_self,
    w_neigh,
    grad_out,
):
    block_rows, width = features.shape
    sub_tiles, slots, tile, _ = band_adj.shape
    hidden = w_self.shape[1]
    blocks = block_rows // tile
    n_feat = lax.axis_size("feat")
    n_node = lax.axis_size("node")
    far_slots = far_adj.shape[3]
    sub_rows = sub_tiles * tile
    half = blocks // 2
    node = lax.axis_index("node")
    member = lax.axis_index("feat")
    h = member % 2
    even = node % 2 == 0
    in_pairs = [(i, i ^ 1) for i in range(n_node)]
    cross_of = [(i + 1) % n_node if i % 2 else (i - 1) % n_node for i in range(n_node)]
    cross_pairs = list(enumerate(cross_of))
    feat_pairs = [(i, i ^ 1) for i in range(n_feat)]

    def dist(k):
        return [(i, (i + k) % n_node) for i in range(n_node)]

    tiles = features.reshape(blocks, tile, width)
    far_c = far_cols.reshape(n_node, far_slots)
    far_r = far_rows.reshape(n_node, far_slots)
    live = far_live.reshape(n_node)
    fadj = far_adj.reshape(n_node, far_slots, tile, tile)
    here = node.reshape(1)
    smem = pl.BlockSpec(memory_space=pltpu.SMEM)
    whole = pl.BlockSpec(memory_space=pltpu.VMEM)

    far_len = -(-far_slots // 16) * 16 + far_slots * tile
    parts = pl.pallas_call(
        functools.partial(far_kernel, far_slots, n_node),
        out_shape=[jax.ShapeDtypeStruct((far_len, width), BF16)] * n_node,
        in_specs=[smem] * 4 + [whole] * 2,
        out_specs=[whole] * n_node,
        compiler_params=pltpu.CompilerParams(vmem_limit_bytes=32 * 1024 * 1024),
        name="far_partial",
    )(far_c, far_r, live, here, tiles, fadj)
    got = [parts[0]] + [lax.ppermute(parts[k], "node", dist(k)) for k in range(1, n_node)]
    rows = jnp.stack(
        [g[far_slots * tile : far_slots * tile + far_slots, 0].astype(jnp.int32) for g in got]
    )

    from_in = lax.ppermute(tiles, "node", in_pairs)
    n_pieces = 2
    each = half // n_pieces
    direct, relayed = [], []
    for i in range(n_pieces):
        piece = lax.dynamic_slice_in_dim(tiles, h * half + i * each, each, 0)
        if i:
            piece, _ = lax.optimization_barrier((piece, parts[0]))
        direct.append(lax.ppermute(piece, "node", cross_pairs))
    for piece in direct:
        relayed.append(lax.ppermute(piece, "feat", feat_pairs))

    kind, local = band_cols // blocks, band_cols % blocks
    is_in = kind == jnp.where(even, 2, 0)
    cross_place = 2 * blocks + ((local // half) ^ h) * half + local % half
    place = jnp.where(kind == 1, local, jnp.where(is_in, blocks + local, cross_place))
    spots = [member * sub_tiles]
    for d in range(n_feat):
        first = (member ^ d) * sub_tiles
        spots.append(2 * blocks + ((first // half) ^ h) * half + first % half)
    spot = jnp.stack(spots).astype(jnp.int32)

    cross_in = direct + relayed
    n_cross = len(cross_in)
    vmem = lambda shape: pl.BlockSpec(shape, lambda t, *_: (0,) * len(shape))
    any_spec = pl.BlockSpec(memory_space=pl.ANY)
    far_shape = (far_slots, tile, width)
    dims = (blocks, slots, n_cross, n_feat, far_slots, n_node)
    results = pl.pallas_call(
        functools.partial(main_kernel, dims),
        out_shape=[
            jax.ShapeDtypeStruct((sub_rows, hidden), BF16),
            jax.ShapeDtypeStruct((sub_rows, width), F32),
            jax.ShapeDtypeStruct((width, hidden), F32),
            jax.ShapeDtypeStruct((width, hidden), F32),
            jax.ShapeDtypeStruct((blocks, tile, width), F32),
            jax.ShapeDtypeStruct((blocks, tile, width), BF16),
        ]
        + [jax.ShapeDtypeStruct((sub_tiles, tile, width), BF16)] * n_feat
        + [jax.ShapeDtypeStruct(far_shape, BF16)] * n_node,
        grid_spec=pltpu.PrefetchScalarGridSpec(
            num_scalar_prefetch=3,
            grid=(sub_tiles,),
            in_specs=[any_spec] * (2 + n_cross)
            + [vmem((far_len, width))] * n_node
            + [
                pl.BlockSpec((1, slots, tile, tile), lambda t, *_: (t, 0, 0, 0)),
                pl.BlockSpec((1, 1, tile), lambda t, *_: (t, 0, 0)),
                vmem((width, hidden)),
                vmem((width, hidden)),
                pl.BlockSpec((tile, hidden), lambda t, *_: (t, 0)),
            ],
            out_specs=[
                pl.BlockSpec((tile, hidden), lambda t, *_: (t, 0)),
                pl.BlockSpec((tile, width), lambda t, *_: (t, 0)),
                vmem((width, hidden)),
                vmem((width, hidden)),
                vmem((blocks, tile, width)),
                vmem((blocks, tile, width)),
            ]
            + [vmem((sub_tiles, tile, width))] * n_feat
            + [vmem(far_shape)] * n_node,
            scratch_shapes=[
                pltpu.VMEM((3 * blocks, tile, width), BF16),
                pltpu.VMEM((3 * blocks, tile, width), F32),
                pltpu.VMEM((sub_tiles, tile, width), BF16),
                pltpu.VMEM((tile, width), F32),
                pltpu.SemaphoreType.DMA((2 + n_cross,)),
            ],
        ),
        compiler_params=pltpu.CompilerParams(vmem_limit_bytes=58 * 1024 * 1024),
        name="layer",
    )(
        place,
        rows,
        spot,
        tiles,
        from_in,
        *cross_in,
        *got,
        band_adj,
        degree.reshape(sub_tiles, 1, tile),
        w_self,
        w_neigh,
        grad_out,
    )
    layer_out, self_back, part_self, part_neigh, own_wide, in_wide = results[:6]
    cross_wide = results[6 : 6 + n_feat]
    send_back = results[6 + n_feat :]

    returned = [send_back[0]] + [
        lax.ppermute(send_back[k], "node", dist(n_node - k)) for k in range(1, n_node)
    ]
    in_terms = lax.ppermute(in_wide, "node", in_pairs)
    odd_first = sorted(range(n_feat), key=lambda d: ((d & -d) if d else n_feat, -d))
    cross_terms = {}
    for i, d in enumerate(odd_first):
        outgoing = cross_wide[d]
        if i:
            outgoing, _ = lax.optimization_barrier((outgoing, returned[min(i, n_node - 1)]))
        cross_terms[d] = lax.ppermute(outgoing, "node", cross_pairs)
    grad_scale = 1.0 / math.sqrt(block_rows * n_node)
    base = pl.pallas_call(
        functools.partial(join_kernel, far_slots, n_node),
        out_shape=jax.ShapeDtypeStruct((blocks, tile, width), F32),
        in_specs=[smem] * 3
        + [pl.BlockSpec(memory_space=pltpu.VMEM)] * (3 + n_node),
        out_specs=pl.BlockSpec(memory_space=pltpu.VMEM),
        compiler_params=pltpu.CompilerParams(vmem_limit_bytes=40 * 1024 * 1024),
        name="join",
    )(far_c, live, here, own_wide, in_terms, fadj, *returned)

    both, _ = lax.optimization_barrier(
        (jnp.concatenate([part_self, part_neigh], 0), base)
    )
    both = summed(both, node, member, n_node, n_feat)
    both = both * grad_scale

    total = self_back.reshape(sub_tiles, tile, width)
    extra = [[] for _ in range(n_feat)]
    sent = None
    for d in odd_first:
        cross = cross_terms[d]
        if sent is not None:
            cross, _ = lax.optimization_barrier((cross, sent))
        chunk = lax.dynamic_slice_in_dim(base, (member ^ d) * sub_tiles, sub_tiles, 0)
        chunk = chunk + cross.astype(F32)
        for term in extra[d]:
            chunk = chunk + term.astype(F32)
        if d == 0:
            total = total + chunk
            break
        sent = chunk.astype(BF16)
        step = d & -d
        extra[d ^ step].append(
            lax.ppermute(sent, "feat", [(i, i ^ step) for i in range(n_feat)])
        )
    return (
        layer_out,
        total.reshape(sub_rows, width),
        both[:width],
        both[width:],
    )


def solution(mesh):
    placed = (
        P(("grp", "node"), None),
        P(("grp", "node", "feat"), None),
        P(("grp", "node", "feat"), None, None, None),
        P(("grp", "node"), "feat", None, None),
        P(("grp", "node"), "feat", None, None),
        P(("grp", "node"), "feat", None),
        P(("grp", "node"), "feat", None, None, None, None),
        P(("grp", "node", "feat")),
        P(),
        P(),
        P(("grp", "node", "feat"), None),
    )
    return jax.shard_map(
        shards,
        mesh=mesh,
        in_specs=placed,
        out_specs=(
            P(("grp", "node", "feat"), None),
            P(("grp", "node", "feat"), None),
            P("grp", None),
            P("grp", None),
        ),
        check_vma=False,
    )
```

```python
import functools
import math

import jax
import jax.numpy as jnp
from jax import lax
from jax.experimental import pallas as pl
from jax.experimental.pallas import tpu as pltpu
from jax.sharding import PartitionSpec as P

F32 = jnp.float32
BF16 = jnp.bfloat16


def outer(a, b):
    return lax.dot_general(a, b, (((0,), (0,)), ((), ())), preferred_element_type=F32)


def times_t(a, b):
    return lax.dot_general(a, b, (((1,), (1,)), ((), ())), preferred_element_type=F32)


def far_kernel(slots, n_node, cols, rows, live, node, feat_ref, adj_ref, *outs):
    tile, width = feat_ref.shape[1:]
    for k, out_ref in enumerate(outs):
        p = lax.rem(node[0] + k, n_node)
        for s in range(slots):
            value = jnp.dot(
                adj_ref[p, s].astype(BF16), feat_ref[cols[p, s]], preferred_element_type=F32
            )
            out_ref[s * tile : (s + 1) * tile] = jnp.where(s < live[p], value, 0.0).astype(BF16)
        line = lax.broadcasted_iota(jnp.int32, (16, width), 0)
        named = jnp.zeros((16, width), F32)
        for s in range(slots):
            named = jnp.where(line == s, rows[p, s].astype(F32), named)
        out_ref[slots * tile :] = named.astype(BF16)


def main_kernel(
    dims,
    cols,
    rows,
    spot,
    own_hbm,
    in_hbm,
    *rest,
):
    blocks, slots, n_cross, n_feat, n_far, n_parts = dims
    cross_hbm, rest = rest[:n_cross], rest[n_cross:]
    part_refs, rest = rest[:n_parts], rest[n_parts:]
    adj_ref, deg_ref, ws_ref, wn_ref, go_ref = rest[:5]
    rest = rest[5:]
    out_ref, self_ref, gs_ref, gn_ref, own_ref, in_ref = rest[:6]
    rest = rest[6:]
    cross_refs, rest = rest[:n_feat], rest[n_feat:]
    send_refs, rest = rest[:n_parts], rest[n_parts:]
    ext, wide, back, acc, sems = rest
    t = pl.program_id(0)
    last = pl.num_programs(0) - 1
    sub = blocks // n_feat

    @pl.when(t == 0)
    def _():
        moves = [
            pltpu.make_async_copy(own_hbm, ext.at[pl.ds(0, blocks)], sems.at[0]),
            pltpu.make_async_copy(in_hbm, ext.at[pl.ds(blocks, blocks)], sems.at[1]),
        ]
        each = blocks // n_cross
        for i, ref in enumerate(cross_hbm):
            moves.append(
                pltpu.make_async_copy(ref, ext.at[pl.ds(2 * blocks + i * each, each)], sems.at[2 + i])
            )
        for move in moves:
            move.start()
        wide[...] = jnp.zeros_like(wide)
        gs_ref[...] = jnp.zeros_like(gs_ref)
        gn_ref[...] = jnp.zeros_like(gn_ref)
        for move in moves:
            move.wait()

    adj = [adj_ref[0, s].astype(BF16) for s in range(slots)]
    near = None
    for s in range(0, slots, 2):
        left = jnp.concatenate([adj[s], adj[s + 1]], axis=1)
        right = jnp.concatenate([ext[cols[t, s]], ext[cols[t, s + 1]]], axis=0)
        term = jnp.dot(left, right, preferred_element_type=F32)
        near = term if near is None else near + term
    acc[...] = near
    for k, ref in enumerate(part_refs):
        for s in range(n_far):

            @pl.when(rows[k, s] == t)
            def _():
                acc[...] += ref[s * acc.shape[0] : (s + 1) * acc.shape[0]].astype(F32)

    deg = jnp.broadcast_to(deg_ref[0].astype(F32), (deg_ref.shape[2], deg_ref.shape[2])).T
    deg = jnp.concatenate([deg, deg], axis=1)
    agg = (acc[...] / deg).astype(BF16)
    mine = ext[spot[0] + t]
    pre = jnp.dot(mine, ws_ref[...], preferred_element_type=F32) + jnp.dot(
        agg, wn_ref[...], preferred_element_type=F32
    )
    sig = jax.nn.sigmoid(pre)
    out_ref[...] = (pre * sig).astype(BF16)
    gz = (go_ref[...].astype(F32) * (sig * (1.0 + pre * (1.0 - sig)))).astype(BF16)
    gs_ref[...] += outer(mine, gz)
    gn_ref[...] += outer(agg, gz)
    bk = (times_t(gz, wn_ref[...]) / deg).astype(BF16)
    self_ref[...] = times_t(gz, ws_ref[...])
    back[t] = bk
    for s in range(slots):
        wide[cols[t, s]] += outer(adj[s], bk)

    @pl.when(t == last)
    def _():
        own_ref[...] = wide[pl.ds(0, blocks)]
        in_ref[...] = wide[pl.ds(blocks, blocks)].astype(BF16)
        for d in range(n_feat):
            cross_refs[d][...] = wide[pl.ds(spot[1 + d], sub)].astype(BF16)
        for k in range(n_parts):
            for s in range(n_far):
                send_refs[k][s] = back[rows[k, s]]


def join_kernel(slots, n_parts, cols, live, node, own_ref, in_ref, adj_ref, *rest):
    ret_refs, out_ref = rest[:n_parts], rest[n_parts]
    out_ref[...] = own_ref[...] + in_ref[...].astype(F32)
    for k in range(n_parts):
        p = lax.rem(node[0] + k, n_parts)
        for s in range(slots):

            @pl.when(s < live[p])
            def _():
                out_ref[cols[p, s]] += outer(adj_ref[p, s].astype(BF16), ret_refs[k][s])


def summed(value, gates, node, member, n_node, n_feat):
    rounds = [("node", node, n_node), ("feat", member, n_feat)]
    for (axis, at, size), gate in zip(rounds, gates):
        value, _ = lax.optimization_barrier((value, gate))
        half = value.shape[0] // 2
        bit = at % 2
        pairs = [(i, i ^ 1) for i in range(size)]
        away = lax.dynamic_slice_in_dim(value, (1 - bit) * half, half, 0)
        kept = lax.dynamic_slice_in_dim(value, bit * half, half, 0)
        value = kept + lax.ppermute(away, axis, pairs)
    value, *_ = lax.optimization_barrier((value, *gates[2:]))
    for axis, size in (("feat", n_feat), ("node", n_node)):
        step = 2
        while step < size:
            value = value + lax.ppermute(value, axis, [(i, i ^ step) for i in range(size)])
            step *= 2
    for axis, at, size in rounds[::-1]:
        other = lax.ppermute(value, axis, [(i, i ^ 1) for i in range(size)])
        first = at % 2 == 0
        value = jnp.concatenate(
            [jnp.where(first, value, other), jnp.where(first, other, value)], axis=0
        )
    return value


def shards(
    features,
    band_cols,
    band_adj,
    far_cols,
    far_rows,
    far_live,
    far_adj,
    degree,
    w_self,
    w_neigh,
    grad_out,
):
    block_rows, width = features.shape
    sub_tiles, slots, tile, _ = band_adj.shape
    hidden = w_self.shape[1]
    blocks = block_rows // tile
    n_feat = lax.axis_size("feat")
    n_node = lax.axis_size("node")
    far_slots = far_adj.shape[3]
    sub_rows = sub_tiles * tile
    half = blocks // 2
    node = lax.axis_index("node")
    member = lax.axis_index("feat")
    h = member % 2
    even = node % 2 == 0
    in_pairs = [(i, i ^ 1) for i in range(n_node)]
    cross_of = [(i + 1) % n_node if i % 2 else (i - 1) % n_node for i in range(n_node)]
    cross_pairs = list(enumerate(cross_of))
    feat_pairs = [(i, i ^ 1) for i in range(n_feat)]

    def dist(k):
        return [(i, (i + k) % n_node) for i in range(n_node)]

    tiles = features.reshape(blocks, tile, width)
    far_c = far_cols.reshape(n_node, far_slots)
    far_r = far_rows.reshape(n_node, far_slots)
    live = far_live.reshape(n_node)
    fadj = far_adj.reshape(n_node, far_slots, tile, tile)
    here = node.reshape(1)
    smem = pl.BlockSpec(memory_space=pltpu.SMEM)
    whole = pl.BlockSpec(memory_space=pltpu.VMEM)

    far_len = -(-far_slots // 16) * 16 + far_slots * tile
    parts = pl.pallas_call(
        functools.partial(far_kernel, far_slots, n_node),
        out_shape=[jax.ShapeDtypeStruct((far_len, width), BF16)] * n_node,
        in_specs=[smem] * 4 + [whole] * 2,
        out_specs=[whole] * n_node,
        compiler_params=pltpu.CompilerParams(vmem_limit_bytes=32 * 1024 * 1024),
        name="far_partial",
    )(far_c, far_r, live, here, tiles, fadj)
    got = [parts[0]] + [lax.ppermute(parts[k], "node", dist(k)) for k in range(1, n_node)]
    rows = jnp.stack(
        [g[far_slots * tile : far_slots * tile + far_slots, 0].astype(jnp.int32) for g in got]
    )

    from_in = lax.ppermute(tiles, "node", in_pairs)
    n_pieces = 2
    each = half // n_pieces
    direct, relayed = [], []
    for i in range(n_pieces):
        piece = lax.dynamic_slice_in_dim(tiles, h * half + i * each, each, 0)
        if i:
            piece, _ = lax.optimization_barrier((piece, parts[0]))
        direct.append(lax.ppermute(piece, "node", cross_pairs))
    for piece in direct:
        relayed.append(lax.ppermute(piece, "feat", feat_pairs))

    kind, local = band_cols // blocks, band_cols % blocks
    is_in = kind == jnp.where(even, 2, 0)
    cross_place = 2 * blocks + ((local // half) ^ h) * half + local % half
    place = jnp.where(kind == 1, local, jnp.where(is_in, blocks + local, cross_place))
    spots = [member * sub_tiles]
    for d in range(n_feat):
        first = (member ^ d) * sub_tiles
        spots.append(2 * blocks + ((first // half) ^ h) * half + first % half)
    spot = jnp.stack(spots).astype(jnp.int32)

    cross_in = direct + relayed
    n_cross = len(cross_in)
    vmem = lambda shape: pl.BlockSpec(shape, lambda t, *_: (0,) * len(shape))
    any_spec = pl.BlockSpec(memory_space=pl.ANY)
    far_shape = (far_slots, tile, width)
    dims = (blocks, slots, n_cross, n_feat, far_slots, n_node)
    results = pl.pallas_call(
        functools.partial(main_kernel, dims),
        out_shape=[
            jax.ShapeDtypeStruct((sub_rows, hidden), BF16),
            jax.ShapeDtypeStruct((sub_rows, width), F32),
            jax.ShapeDtypeStruct((width, hidden), F32),
            jax.ShapeDtypeStruct((width, hidden), F32),
            jax.ShapeDtypeStruct((blocks, tile, width), F32),
            jax.ShapeDtypeStruct((blocks, tile, width), BF16),
        ]
        + [jax.ShapeDtypeStruct((sub_tiles, tile, width), BF16)] * n_feat
        + [jax.ShapeDtypeStruct(far_shape, BF16)] * n_node,
        grid_spec=pltpu.PrefetchScalarGridSpec(
            num_scalar_prefetch=3,
            grid=(sub_tiles,),
            in_specs=[any_spec] * (2 + n_cross)
            + [vmem((far_len, width))] * n_node
            + [
                pl.BlockSpec((1, slots, tile, tile), lambda t, *_: (t, 0, 0, 0)),
                pl.BlockSpec((1, 1, tile), lambda t, *_: (t, 0, 0)),
                vmem((width, hidden)),
                vmem((width, hidden)),
                pl.BlockSpec((tile, hidden), lambda t, *_: (t, 0)),
            ],
            out_specs=[
                pl.BlockSpec((tile, hidden), lambda t, *_: (t, 0)),
                pl.BlockSpec((tile, width), lambda t, *_: (t, 0)),
                vmem((width, hidden)),
                vmem((width, hidden)),
                vmem((blocks, tile, width)),
                vmem((blocks, tile, width)),
            ]
            + [vmem((sub_tiles, tile, width))] * n_feat
            + [vmem(far_shape)] * n_node,
            scratch_shapes=[
                pltpu.VMEM((3 * blocks, tile, width), BF16),
                pltpu.VMEM((3 * blocks, tile, width), F32),
                pltpu.VMEM((sub_tiles, tile, width), BF16),
                pltpu.VMEM((tile, width), F32),
                pltpu.SemaphoreType.DMA((2 + n_cross,)),
            ],
        ),
        compiler_params=pltpu.CompilerParams(vmem_limit_bytes=58 * 1024 * 1024),
        name="layer",
    )(
        place,
        rows,
        spot,
        tiles,
        from_in,
        *cross_in,
        *got,
        band_adj,
        degree.reshape(sub_tiles, 1, tile),
        w_self,
        w_neigh,
        grad_out,
    )
    layer_out, self_back, part_self, part_neigh, own_wide, in_wide = results[:6]
    cross_wide = results[6 : 6 + n_feat]
    send_back = results[6 + n_feat :]

    in_terms = lax.ppermute(in_wide, "node", in_pairs)
    odd_first = sorted(range(n_feat), key=lambda d: ((d & -d) if d else n_feat, -d))
    cross_terms = {}

    for d in odd_first:
        outgoing = cross_wide[d]
        cross_terms[d] = lax.ppermute(outgoing, "node", cross_pairs)
    returned = [send_back[0]] + [
        lax.ppermute(send_back[k], "node", dist(n_node - k)) for k in range(1, n_node)
    ]
    grad_scale = 1.0 / math.sqrt(block_rows * n_node)
    both = jnp.concatenate([part_self, part_neigh], 0)
    gates = [cross_terms[d] for d in odd_first]
    both = summed(both, gates, node, member, n_node, n_feat)
    both = both * grad_scale

    base = pl.pallas_call(
        functools.partial(join_kernel, far_slots, n_node),
        out_shape=jax.ShapeDtypeStruct((blocks, tile, width), F32),
        in_specs=[smem] * 3
        + [pl.BlockSpec(memory_space=pltpu.VMEM)] * (3 + n_node),
        out_specs=pl.BlockSpec(memory_space=pltpu.VMEM),
        compiler_params=pltpu.CompilerParams(vmem_limit_bytes=40 * 1024 * 1024),
        name="join",
    )(far_c, live, here, own_wide, in_terms, fadj, *returned)

    total = self_back.reshape(sub_tiles, tile, width)
    extra = [[] for _ in range(n_feat)]
    sent = None
    for d in odd_first:
        cross = cross_terms[d]
        if sent is not None:
            cross, _ = lax.optimization_barrier((cross, sent))
        chunk = lax.dynamic_slice_in_dim(base, (member ^ d) * sub_tiles, sub_tiles, 0)
        chunk = chunk + cross.astype(F32)
        for term in extra[d]:
            chunk = chunk + term.astype(F32)
        if d == 0:
            total = total + chunk
            break
        sent = chunk.astype(BF16)
        step = d & -d
        extra[d ^ step].append(
            lax.ppermute(sent, "feat", [(i, i ^ step) for i in range(n_feat)])
        )
    return (
        layer_out,
        total.reshape(sub_rows, width),
        both[:width],
        both[width:],
    )


def solution(mesh):
    placed = (
        P(("grp", "node"), None),
        P(("grp", "node", "feat"), None),
        P(("grp", "node", "feat"), None, None, None),
        P(("grp", "node"), "feat", None, None),
        P(("grp", "node"), "feat", None, None),
        P(("grp", "node"), "feat", None),
        P(("grp", "node"), "feat", None, None, None, None),
        P(("grp", "node", "feat")),
        P(),
        P(),
        P(("grp", "node", "feat"), None),
    )
    return jax.shard_map(
        shards,
        mesh=mesh,
        in_specs=placed,
        out_specs=(
            P(("grp", "node", "feat"), None),
            P(("grp", "node", "feat"), None),
            P("grp", None),
            P("grp", None),
        ),
        check_vma=False,
    )
```
